768 devices in a mesh: row: 16 (over x, z_hi), col: 48 (over y, z_lo, core).
Axes of the slice: x: 4, y: 8, z: 12 (z_hi: 4, z_lo: 3; z = z_hi * 3 + z_lo), core: 2. Of those that a mesh axis runs over, the one named last changes fastest.
Arguments:
- data: float32 [24576, 36864], P('row', 'col'), may hold values from 0.1 to 10
- w_factor: float32 [24576, 128], P(('row', 'col')), may hold values from 0.01 to 1
- h_factor: float32 [36864, 128], P(('col', 'row')), may hold values from 0.01 to 1
Outputs:
- w_final: float32 [24576, 128], P(('row', 'col'))
- h_final: float32 [36864, 128], P(('col', 'row'))
The draws below stay inside these ranges and needn't reach their ends.
All inputs are finite; a program needn't handle non-finite values.
Results may differ from the reference program's by a relative error of at most 0.0003.
Values sent between devices are 32-bit elements; how exact they have to be, the bound alone decides.
No kernel may reach another device: no remote copies, remote signals or barrier semaphores. Data moves between devices by JAX's collectives and lax.ppermute only.
A program may use at most 32 MiB of HBM per device.

```python
import math
import jax
import jax.numpy as jnp
from jax import lax

K = 128
TILE_M = 1536
ITERS = 2
M = 24576
N = 36864
N_ROW = 16


def shard_levels(stream_key, extent, cuts, least, largest):
    def one(dim, parts):
        steps = jax.random.uniform(jax.random.fold_in(jax.random.fold_in(stream_key, 6), dim), (parts,), jnp.float32, least / len(cuts), largest / len(cuts))
        return jnp.repeat(jnp.exp(steps), extent[dim] // parts).reshape((-1,) + (1,) * (len(extent) - dim - 1))

    loudness = one(*cuts[0])
    for cut in cuts[1:]:
        loudness = loudness * one(*cut)
    return loudness


def setup_inputs(seed: int = 0) -> dict:
    splits = jax.random.split(jax.random.key(seed), 4)
    data = jnp.clip(jnp.exp(math.log(10.0) - 4.6051702 * jax.random.uniform(splits[0], (M, N), jnp.float32) ** shard_levels(splits[0], (M, N), ((0, 16), (1, 48)), -0.2, 0.2)), 0.1, 10.0)
    w_factor = jnp.clip(jnp.exp(math.log(1.0) - 4.6051702 * jax.random.uniform(splits[1], (M, K), jnp.float32) ** shard_levels(splits[1], (M, K), ((0, 768),), -0.2, 0.2)), 0.01, 1.0)
    h_factor = jnp.clip(jnp.exp(math.log(1.0) - 4.6051702 * jax.random.uniform(splits[2], (N, K), jnp.float32) ** shard_levels(splits[2], (N, K), ((0, 768),), -0.2, 0.2)), 0.01, 1.0)
    return {"data": data, "w_factor": w_factor, "h_factor": h_factor}


HIGH = lax.Precision.HIGHEST


def update_h(blocks, w_blocks, h_cur):
    def step(total, pair):
        block, w_block = pair
        model = jnp.dot(w_block, h_cur.T, precision=HIGH, preferred_element_type=jnp.float32)
        ratio = block / model
        return total + jnp.dot(ratio.T, w_block, precision=HIGH, preferred_element_type=jnp.float32), None
    numer, unused = lax.scan(step, jnp.zeros(h_cur.shape, jnp.float32), (blocks, w_blocks))
    wsum = jnp.sum(w_blocks, axis=(0, 1))
    return h_cur * numer / wsum


def update_w(blocks, w_blocks, h_cur):
    hsum = jnp.sum(h_cur, axis=0)

    def one_block(pair):
        block, w_block = pair
        model = jnp.dot(w_block, h_cur.T, precision=HIGH, preferred_element_type=jnp.float32)
        ratio = block / model
        return w_block * jnp.dot(ratio, h_cur, precision=HIGH, preferred_element_type=jnp.float32) / hsum
    return lax.map(one_block, (blocks, w_blocks))


def reference(data, w_factor, h_factor):
    blocks = data.reshape(N_ROW, TILE_M, N)
    w_blocks = w_factor.reshape(N_ROW, TILE_M, K)
    h_cur = h_factor
    for step in range(ITERS):
        h_cur = update_h(blocks, w_blocks, h_cur)
        w_blocks = update_w(blocks, w_blocks, h_cur)
    return w_blocks.reshape(M, K), h_cur
```

```python
import functools

import jax
import jax.numpy as jnp
from jax import lax
from jax.experimental import pallas as pl
from jax.experimental.pallas import tpu as pltpu
from jax.sharding import Mesh, PartitionSpec as P

ITERS = 2
X, ZH, Y, ZL, C = 4, 4, 8, 3, 2
COL = ("zl", "y")
PAD = 8
H_PIECE, W_PIECE = 512, 256
VMEM = 48 * 2**20


def split(a):
    high = a.astype(jnp.bfloat16)
    return high, (a - high.astype(jnp.float32)).astype(jnp.bfloat16)


def half_kernel(read, piece, groups, which_ref, d_ref, a_ref, b_ref, o_ref, b_wide, b_pair, b_sum):
    n, k = b_ref.shape

    @pl.when(pl.program_id(0) == 0)
    def _():
        b = b_ref[...]
        high, low = split(b.T)
        b_wide[...] = jnp.concatenate([high, high, low], axis=0)
        b_pair[...] = jnp.concatenate(split(b), axis=1)
        b_sum[...] = jnp.broadcast_to(jnp.sum(b, axis=0, keepdims=True), (PAD, k))

    rows = a_ref.shape[0]
    high, low = split(a_ref[...])
    a_wide = jnp.concatenate([high, low, high], axis=1)
    total = jnp.zeros((rows, 2 * k), jnp.float32)
    for at in range(0, n, piece):
        cols = pl.ds(at, piece)
        model = jnp.dot(a_wide, b_wide[:, cols], preferred_element_type=jnp.float32)
        guess = pltpu.reciprocal(model, approx=True)
        high, low = split(read(d_ref, cols) * (guess * (2.0 - model * guess)))
        pair = b_pair[cols, :]
        total += jnp.dot(high, pair, preferred_element_type=jnp.float32)
        total += jnp.dot(low, pair, preferred_element_type=jnp.float32)
    numer = total[:, :k] + total[:, k:]
    each = rows // groups
    for g in range(groups):
        o_ref[g, 0:each, :] = numer[g * each : (g + 1) * each]
        o_ref[g, each : each + PAD, :] = b_sum[...]


def half(read, piece, d, d_spec, a, a_spec, b, rows, steps, groups, which):
    n, k = b.shape
    each = rows // groups
    return pl.pallas_call(
        functools.partial(half_kernel, read, piece, groups),
        grid_spec=pltpu.PrefetchScalarGridSpec(
            num_scalar_prefetch=1,
            grid=(steps,),
            in_specs=[d_spec, a_spec, pl.BlockSpec((n, k), lambda i, c: (0, 0))],
            out_specs=pl.BlockSpec((groups, each + PAD, k), lambda i, c: (i, 0, 0)),
            scratch_shapes=[
                pltpu.VMEM((3 * k, n), jnp.bfloat16),
                pltpu.VMEM((n, 2 * k), jnp.bfloat16),
                pltpu.VMEM((PAD, k), jnp.float32),
            ],
        ),
        out_shape=jax.ShapeDtypeStruct((steps * groups, each + PAD, k), jnp.float32),
        compiler_params=pltpu.CompilerParams(vmem_limit_bytes=VMEM),
        cost_estimate=pl.CostEstimate(
            flops=12 * steps * rows * n * k, bytes_accessed=4 * steps * rows * n, transcendentals=0
        ),
    )(which, d, a, b)


H_STEPS = 1


def half_h(dt, h_panel, w_panel):
    n, m = dt.shape
    rows = n // H_STEPS
    return half(
        lambda ref, cols: ref[:, cols],
        H_PIECE,
        dt,
        pl.BlockSpec((rows, m), lambda i, c: (i, 0)),
        h_panel,
        pl.BlockSpec((rows, h_panel.shape[1]), lambda i, c: (i, 0)),
        w_panel,
        rows,
        H_STEPS,
        X // H_STEPS,
        jnp.zeros((1,), jnp.int32),
    )


W_STEPS = 1


def half_w(d5, w_panel, h_panel, core):
    rows, n = d5.shape[3], d5.shape[4]
    own = ZL // W_STEPS
    block = own * Y * rows

    def read(ref, cols):
        part = ref[:, :, 0, :, cols]
        return jnp.swapaxes(part, 0, 1).reshape(block, -1)

    return half(
        read,
        W_PIECE,
        d5,
        pl.BlockSpec((Y, own, 1, rows, n), lambda i, c: (0, i, c[0], 0, 0)),
        w_panel,
        pl.BlockSpec((block, w_panel.shape[1]), lambda i, c: (c[0] * W_STEPS + i, 0)),
        h_panel,
        block,
        W_STEPS,
        own * Y,
        core.astype(jnp.int32).reshape(1),
    )


def turn_kernel(d_ref, o_ref):
    n = d_ref.shape[-1]
    o_ref[...] = d_ref[...].reshape(-1, n).T


def turned(d5):
    rows, n = d5.shape[3], d5.shape[4]
    return pl.pallas_call(
        turn_kernel,
        grid=(C * ZL,),
        in_specs=[pl.BlockSpec((Y, 1, 1, rows, n), lambda i: (0, i % ZL, i // ZL, 0, 0))],
        out_specs=pl.BlockSpec((n, Y * rows), lambda i: (0, i)),
        out_shape=jax.ShapeDtypeStruct((n, C * ZL * Y * rows), jnp.float32),
        compiler_params=pltpu.CompilerParams(vmem_limit_bytes=VMEM),
        cost_estimate=pl.CostEstimate(flops=0, bytes_accessed=8 * d5.size, transcendentals=0),
    )(d5)


def exchange(chunks, axes):
    return lax.all_to_all(chunks, axes, 0, 0, tiled=True)


def spread(part, axes, n):
    whole = exchange(jnp.broadcast_to(part[None], (n,) + part.shape), axes)
    return whole.reshape((-1,) + part.shape[1:])


def gather_w(w):
    return lax.all_gather(spread(w, COL, ZL * Y), "c", axis=0, tiled=True)


def on_device(data, w, h):
    w_rows, h_rows = w.shape[0], h.shape[0]
    d5 = data.reshape(Y, ZL, C, w_rows, data.shape[1])
    core = lax.axis_index("c")
    h_x = lax.all_gather(h, "zh", axis=0, tiled=True)
    dt = turned(d5)
    h_panel = spread(h_x, "x", X)
    for step in range(ITERS):
        w_panel = gather_w(w)
        part = half_h(dt, h_panel, w_panel)
        part = jnp.sum(exchange(part, "x"), axis=0)
        part = jnp.sum(lax.all_gather(part, "zh", axis=0), axis=0)
        h_x = h_x * part[: ZH * h_rows] / part[ZH * h_rows]
        h_panel = spread(h_x, "x", X)
        sent = lax.ppermute(half_w(d5, w_panel, h_panel, 1 - core), "c", [(0, 1), (1, 0)])
        part = half_w(d5, w_panel, h_panel, core) + sent
        part = jnp.sum(exchange(part, COL), axis=0)
        w = w * part[:w_rows] / part[w_rows]
    return w, lax.dynamic_slice_in_dim(h_x, lax.axis_index("zh") * h_rows, h_rows, 0)


def solution(mesh):
    fine = Mesh(mesh.devices.reshape(X, ZH, Y, ZL, C), ("x", "zh", "y", "zl", "c"))
    row, col = ("x", "zh"), ("y", "zl", "c")
    in_specs = (P(row, col), P(row + col, None), P(col + row, None))
    out_specs = (P(row + col, None), P(col + row, None))
    return jax.shard_map(on_device, mesh=fine, in_specs=in_specs, out_specs=out_specs, check_vma=False)
```

```python
import functools

import jax
import jax.numpy as jnp
from jax import lax
from jax.experimental import pallas as pl
from jax.experimental.pallas import tpu as pltpu
from jax.sharding import Mesh, PartitionSpec as P

ITERS = 2
X, ZH, Y, ZL, C = 4, 4, 8, 3, 2
COL = ("zl", "y")
H_PAD, W_PAD = 8, 1
H_PIECE, W_PIECE = 512, 256
VMEM = 48 * 2**20


def split(a):
    high = a.astype(jnp.bfloat16)
    return high, (a - high.astype(jnp.float32)).astype(jnp.bfloat16)


def half_kernel(read, piece, groups, pad, which_ref, d_ref, a_ref, b_ref, o_ref, b_wide, b_pair):
    n, k = b_ref.shape
    b = b_ref[...]
    high, low = split(b.T)
    b_wide[...] = jnp.concatenate([high, high, low], axis=0)
    b_pair[...] = jnp.concatenate(split(b), axis=1)
    b_sum = jnp.broadcast_to(jnp.sum(b, axis=0, keepdims=True), (pad, k))
    rows = a_ref.shape[0]
    high, low = split(a_ref[...])
    a_wide = jnp.concatenate([high, low, high], axis=1)
    total = jnp.zeros((rows, 2 * k), jnp.float32)
    for at in range(0, n, piece):
        cols = pl.ds(at, piece)
        model = jnp.dot(a_wide, b_wide[:, cols], preferred_element_type=jnp.float32)
        guess = pltpu.reciprocal(model, approx=True)
        high, low = split(read(d_ref, cols) * (guess * (2.0 - model * guess)))
        pair = b_pair[cols, :]
        total += jnp.dot(high, pair, preferred_element_type=jnp.float32)
        total += jnp.dot(low, pair, preferred_element_type=jnp.float32)
    numer = total[:, :k] + total[:, k:]
    each = rows // groups
    for g in range(groups):
        start = g * (each + pad)
        o_ref[pl.ds(start, each), :] = numer[g * each : (g + 1) * each]
        o_ref[pl.ds(start + each, pad), :] = b_sum


def half(read, piece, d, d_spec, a, a_spec, b, groups, pad, which):
    n, k = b.shape
    rows = a_spec.block_shape[0]
    out = (rows + groups * pad, k)
    return pl.pallas_call(
        functools.partial(half_kernel, read, piece, groups, pad),
        grid_spec=pltpu.PrefetchScalarGridSpec(
            num_scalar_prefetch=1,
            grid=(1,),
            in_specs=[d_spec, a_spec, pl.BlockSpec((n, k), lambda i, c: (0, 0))],
            out_specs=pl.BlockSpec(out, lambda i, c: (0, 0)),
            scratch_shapes=[pltpu.VMEM((3 * k, n), jnp.bfloat16), pltpu.VMEM((n, 2 * k), jnp.bfloat16)],
        ),
        out_shape=jax.ShapeDtypeStruct(out, jnp.float32),
        compiler_params=pltpu.CompilerParams(vmem_limit_bytes=VMEM),
        cost_estimate=pl.CostEstimate(flops=12 * rows * n * k, bytes_accessed=4 * rows * n, transcendentals=0),
    )(which, d, a, b)


def half_h(dt, h_panel, w_panel):
    k = h_panel.shape[1]
    d_spec = pl.BlockSpec(dt.shape, lambda i, c: (0, 0))
    spec = pl.BlockSpec(h_panel.shape, lambda i, c: (0, 0))
    unused = jnp.zeros((1,), jnp.int32)
    part = half(lambda ref, cols: ref[:, cols], H_PIECE, dt, d_spec, h_panel, spec, w_panel, X, H_PAD, unused)
    return part.reshape(X, -1, k)


def half_w(d5, w_panel, h_panel, core):
    rows, n = d5.shape[3], d5.shape[4]
    block, k = ZL * Y * rows, w_panel.shape[1]

    def read(ref, cols):
        return jnp.swapaxes(ref[:, :, 0, :, cols], 0, 1).reshape(block, -1)

    d_spec = pl.BlockSpec((Y, ZL, 1, rows, n), lambda i, c: (0, 0, c[0], 0, 0))
    spec = pl.BlockSpec((block, k), lambda i, c: (c[0], 0))
    core = core.astype(jnp.int32).reshape(1)
    return half(read, W_PIECE, d5, d_spec, w_panel, spec, h_panel, ZL * Y, W_PAD, core)


def update_kernel(copies, parts_ref, w_ref, o_ref, *copies_ref):
    rows = w_ref.shape[0]
    each = rows + W_PAD
    total = parts_ref[pl.ds(0, each), :]
    for g in range(1, copies):
        total += parts_ref[pl.ds(g * each, each), :]
    w = w_ref[...] * total[:rows] / total[rows : rows + 1]
    o_ref[...] = w
    for ref in copies_ref:
        for g in range(copies):
            ref[g] = w


def update(parts, w, last):
    copies = ZL * Y
    whole = pl.BlockSpec(memory_space=pltpu.VMEM)
    shapes = [jax.ShapeDtypeStruct(w.shape, w.dtype)]
    if not last:
        shapes.append(jax.ShapeDtypeStruct((copies,) + w.shape, w.dtype))
    return pl.pallas_call(
        functools.partial(update_kernel, copies),
        in_specs=[whole, whole],
        out_specs=[whole] * len(shapes),
        out_shape=shapes,
        compiler_params=pltpu.CompilerParams(vmem_limit_bytes=VMEM),
    )(parts, w)


def turn_kernel(d_ref, o_ref):
    n = d_ref.shape[-1]
    o_ref[...] = d_ref[...].reshape(-1, n).T


def turned(d5):
    rows, n = d5.shape[3], d5.shape[4]
    return pl.pallas_call(
        turn_kernel,
        grid=(C * ZL,),
        in_specs=[pl.BlockSpec((Y, 1, 1, rows, n), lambda i: (0, i % ZL, i // ZL, 0, 0))],
        out_specs=pl.BlockSpec((n, Y * rows), lambda i: (0, i)),
        out_shape=jax.ShapeDtypeStruct((n, C * ZL * Y * rows), jnp.float32),
        compiler_params=pltpu.CompilerParams(vmem_limit_bytes=VMEM),
        cost_estimate=pl.CostEstimate(flops=0, bytes_accessed=8 * d5.size, transcendentals=0),
    )(d5)


def exchange(chunks, axes):
    return lax.all_to_all(chunks, axes, 0, 0, tiled=True)


def spread(part, axes, n):
    whole = exchange(jnp.broadcast_to(part[None], (n,) + part.shape), axes)
    return whole.reshape((-1,) + part.shape[1:])


def gather_w(copies):
    whole = exchange(copies, COL).reshape(-1, copies.shape[2])
    return lax.all_gather(whole, "c", axis=0, tiled=True)


def on_device(data, w, h):
    (w_rows, k), h_rows = w.shape, h.shape[0]
    d5 = data.reshape(Y, ZL, C, w_rows, data.shape[1])
    core = lax.axis_index("c")
    w_panel = gather_w(jnp.broadcast_to(w[None], (ZL * Y,) + w.shape))
    dt = turned(d5)
    h_x = lax.all_gather(h, "zh", axis=0, tiled=True)
    h_panel = spread(h_x, "x", X)
    for step in range(ITERS):
        part = half_h(dt, h_panel, w_panel)
        part = jnp.sum(exchange(part, "x"), axis=0)
        part = jnp.sum(lax.all_gather(part, "zh", axis=0), axis=0)
        h_x = h_x * part[: ZH * h_rows] / part[ZH * h_rows]
        h_panel = spread(h_x, "x", X)
        sent = lax.ppermute(half_w(d5, w_panel, h_panel, 1 - core), "c", [(0, 1), (1, 0)])
        part = half_w(d5, w_panel, h_panel, core) + sent
        part = exchange(part.reshape(ZL * Y, 1, -1), COL).reshape(-1, k)
        last = step == ITERS - 1
        w, *copies = update(part, w, last)
        if not last:
            w_panel = gather_w(*copies)
    return w, lax.dynamic_slice_in_dim(h_x, lax.axis_index("zh") * h_rows, h_rows, 0)


def solution(mesh):
    fine = Mesh(mesh.devices.reshape(X, ZH, Y, ZL, C), ("x", "zh", "y", "zl", "c"))
    row, col = ("x", "zh"), ("y", "zl", "c")
    in_specs = (P(row, col), P(row + col, None), P(col + row, None))
    out_specs = (P(row + col, None), P(col + row, None))
    return jax.shard_map(on_device, mesh=fine, in_specs=in_specs, out_specs=out_specs, check_vma=False)
```

```python
import functools

import jax
import jax.numpy as jnp
from jax import lax
from jax.experimental import pallas as pl
from jax.experimental.pallas import tpu as pltpu
from jax.sharding import Mesh, PartitionSpec as P

ITERS = 2
X, ZH, Y, ZL, C = 4, 4, 8, 3, 2
COL = ("zl", "y")
H_PAD, W_PAD = 8, 1
PIECE = 256
H_COPIES = 2
VMEM, TURN_VMEM = 48 * 2**20, 60 * 2**20


def split(a):
    high = a.astype(jnp.bfloat16)
    return high, (a - high.astype(jnp.float32)).astype(jnp.bfloat16)


def half_kernel(fetch, read, groups, pad, which_ref, d_ref, a_ref, b_ref, o_ref, d_all, b_wide, b_pair, sems):
    n, k = b_ref.shape
    rows = o_ref.shape[0] - groups * pad
    which = which_ref[0]
    copies = fetch(which, d_ref, d_all, sems)
    for copy in copies:
        copy.start()
    b = b_ref[...]
    high, low = split(b.T)
    b_wide[...] = jnp.concatenate([high, high, low], axis=0)
    b_pair[...] = jnp.concatenate(split(b), axis=1)
    b_sum = jnp.broadcast_to(jnp.sum(b, axis=0, keepdims=True), (pad, k))
    high, low = split(a_ref[pl.ds(pl.multiple_of(which * rows, rows), rows), :])
    a_wide = jnp.concatenate([high, low, high], axis=1)
    total = jnp.zeros((rows, 2 * k), jnp.float32)
    pieces = [pl.ds(at, PIECE) for at in range(0, n, PIECE)]

    def model_of(cols):
        return jnp.dot(a_wide, b_wide[:, cols], preferred_element_type=jnp.float32)

    later = model_of(pieces[0])
    part = len(pieces) // len(copies)
    for i, cols in enumerate(pieces):
        if i % part == 0:
            copies[i // part].wait()
        model = later
        if i + 1 < len(pieces):
            later = model_of(pieces[i + 1])
        guess = pltpu.reciprocal(model, approx=True)
        high, low = split(read(d_all, cols) * (guess * (2.0 - model * guess)))
        pair = b_pair[cols, :]
        total += jnp.dot(high, pair, preferred_element_type=jnp.float32)
        total += jnp.dot(low, pair, preferred_element_type=jnp.float32)
    numer = total[:, :k] + total[:, k:]
    each = rows // groups
    for g in range(groups):
        start = g * (each + pad)
        o_ref[pl.ds(start, each), :] = numer[g * each : (g + 1) * each]
        o_ref[pl.ds(start + each, pad), :] = b_sum


def half(fetch, read, d, d_shape, a, b, rows, groups, pad, which):
    n, k = b.shape
    whole = pl.BlockSpec(memory_space=pltpu.VMEM)
    return pl.pallas_call(
        functools.partial(half_kernel, fetch, read, groups, pad),
        in_specs=[pl.BlockSpec(memory_space=pltpu.SMEM), pl.BlockSpec(memory_space=pl.ANY), whole, whole],
        out_specs=whole,
        out_shape=jax.ShapeDtypeStruct((rows + groups * pad, k), jnp.float32),
        scratch_shapes=[
            pltpu.VMEM(d_shape, jnp.float32),
            pltpu.VMEM((3 * k, n), jnp.bfloat16),
            pltpu.VMEM((n, 2 * k), jnp.bfloat16),
            pltpu.SemaphoreType.DMA((H_COPIES,)),
        ],
        compiler_params=pltpu.CompilerParams(vmem_limit_bytes=VMEM),
        cost_estimate=pl.CostEstimate(flops=12 * rows * n * k, bytes_accessed=4 * rows * n, transcendentals=0),
    )(which, d, a, b)


def half_h(dt, h_panel, w_panel):
    n, k = h_panel.shape

    def fetch(which, ref, held, sems):
        width = ref.shape[1] // H_COPIES
        parts = [pl.ds(i * width, width) for i in range(H_COPIES)]
        return [pltpu.make_async_copy(ref.at[:, cols], held.at[:, cols], sems.at[i]) for i, cols in enumerate(parts)]

    def read(held, cols):
        return held[:, cols]

    first = jnp.zeros((1,), jnp.int32)
    return half(fetch, read, dt, dt.shape, h_panel, w_panel, n, X, H_PAD, first).reshape(X, -1, k)


def half_w(d5, w_panel, h_panel, core):
    rows, n = d5.shape[3], d5.shape[4]
    block = ZL * Y * rows

    def fetch(which, ref, held, sems):
        return [pltpu.make_async_copy(ref.at[:, :, which], held, sems.at[0])]

    def read(held, cols):
        return jnp.swapaxes(held[:, :, :, cols], 0, 1).reshape(block, -1)

    core = core.astype(jnp.int32).reshape(1)
    return half(fetch, read, d5, (Y, ZL, rows, n), w_panel, h_panel, block, ZL * Y, W_PAD, core)


def update_kernel(copies, parts_ref, w_ref, o_ref, *copies_ref):
    rows = w_ref.shape[0]
    each = rows + W_PAD
    total = parts_ref[pl.ds(0, each), :]
    for g in range(1, copies):
        total += parts_ref[pl.ds(g * each, each), :]
    w = w_ref[...] * total[:rows] / total[rows : rows + 1]
    o_ref[...] = w
    for ref in copies_ref:
        for g in range(copies):
            ref[g] = w


def update(parts, w, last):
    copies = ZL * Y
    whole = pl.BlockSpec(memory_space=pltpu.VMEM)
    shapes = [jax.ShapeDtypeStruct(w.shape, w.dtype)]
    if not last:
        shapes.append(jax.ShapeDtypeStruct((copies,) + w.shape, w.dtype))
    return pl.pallas_call(
        functools.partial(update_kernel, copies),
        in_specs=[whole, whole],
        out_specs=[whole] * len(shapes),
        out_shape=shapes,
        compiler_params=pltpu.CompilerParams(vmem_limit_bytes=VMEM),
    )(parts, w)


def turn_kernel(d_ref, o_ref):
    n = d_ref.shape[-1]
    o_ref[...] = d_ref[...].reshape(-1, n).T


def turned(d5):
    rows, n = d5.shape[3], d5.shape[4]
    return pl.pallas_call(
        turn_kernel,
        grid=(C * ZL,),
        in_specs=[pl.BlockSpec((Y, 1, 1, rows, n), lambda i: (0, i % ZL, i // ZL, 0, 0))],
        out_specs=pl.BlockSpec((n, Y * rows), lambda i: (0, i)),
        out_shape=jax.ShapeDtypeStruct((n, C * ZL * Y * rows), jnp.float32),
        compiler_params=pltpu.CompilerParams(vmem_limit_bytes=TURN_VMEM),
        cost_estimate=pl.CostEstimate(flops=0, bytes_accessed=8 * d5.size, transcendentals=0),
    )(d5)


def exchange(chunks, axes):
    return lax.all_to_all(chunks, axes, 0, 0, tiled=True)


def spread(part, axes, n):
    whole = exchange(jnp.broadcast_to(part[None], (n,) + part.shape), axes)
    return whole.reshape((-1,) + part.shape[1:])


def gather_w(copies):
    whole = exchange(copies, COL).reshape(-1, copies.shape[2])
    return lax.all_gather(whole, "c", axis=0, tiled=True)


def on_device(data, w, h):
    (w_rows, k), h_rows = w.shape, h.shape[0]
    d5 = data.reshape(Y, ZL, C, w_rows, data.shape[1])
    core = lax.axis_index("c")
    w_panel = gather_w(jnp.broadcast_to(w[None], (ZL * Y,) + w.shape))
    dt = turned(d5)
    h_x = lax.all_gather(h, "zh", axis=0, tiled=True)
    h_panel = spread(h_x, "x", X)
    for step in range(ITERS):
        part = half_h(dt, h_panel, w_panel)
        part = jnp.sum(exchange(part, "x"), axis=0)
        part = jnp.sum(lax.all_gather(part, "zh", axis=0), axis=0)
        h_x = h_x * part[: ZH * h_rows] / part[ZH * h_rows]
        h_panel = spread(h_x, "x", X)
        sent = lax.ppermute(half_w(d5, w_panel, h_panel, 1 - core), "c", [(0, 1), (1, 0)])
        part = half_w(d5, w_panel, h_panel, core) + sent
        part = exchange(part.reshape(ZL * Y, 1, -1), COL).reshape(-1, k)
        last = step == ITERS - 1
        w, *copies = update(part, w, last)
        if not last:
            w_panel = gather_w(*copies)
    return w, lax.dynamic_slice_in_dim(h_x, lax.axis_index("zh") * h_rows, h_rows, 0)


def solution(mesh):
    fine = Mesh(mesh.devices.reshape(X, ZH, Y, ZL, C), ("x", "zh", "y", "zl", "c"))
    row, col = ("x", "zh"), ("y", "zl", "c")
    in_specs = (P(row, col), P(row + col, None), P(col + row, None))
    out_specs = (P(row + col, None), P(col + row, None))
    return jax.shard_map(on_device, mesh=fine, in_specs=in_specs, out_specs=out_specs, check_vma=False)
```

```python
import functools

import jax
import jax.numpy as jnp
from jax import lax
from jax.experimental import pallas as pl
from jax.experimental.pallas import tpu as pltpu
from jax.sharding import Mesh, PartitionSpec as P

ITERS = 2
X, ZH, Y, ZL, C = 4, 4, 8, 3, 2
COL = ("zl", "y")
H_PAD, W_PAD = 8, 1
PIECE = 256
H_COPIES = 2
VMEM, TURN_VMEM = 48 * 2**20, 60 * 2**20


def split(a):
    high = a.astype(jnp.bfloat16)
    return high, (a - high.astype(jnp.float32)).astype(jnp.bfloat16)


def half_kernel(fetch, read, groups, pad, which_ref, d_ref, a_ref, b_ref, o_ref, d_all, b_wide, b_pair, sems):
    n, k = b_ref.shape
    rows = o_ref.shape[0] - groups * pad
    which = which_ref[0]
    copies = fetch(which, d_ref, d_all, sems)
    for copy in copies:
        copy.start()
    b = b_ref[...]
    high, low = split(b.T)
    b_wide[...] = jnp.concatenate([high, high, low], axis=0)
    b_pair[...] = jnp.concatenate(split(b), axis=1)
    b_sum = jnp.broadcast_to(jnp.sum(b, axis=0, keepdims=True), (pad, k))
    high, low = split(a_ref[pl.ds(pl.multiple_of(which * rows, rows), rows), :])
    a_wide = jnp.concatenate([high, low, high], axis=1)
    total = jnp.zeros((rows, 2 * k), jnp.float32)
    pieces = [pl.ds(at, PIECE) for at in range(0, n, PIECE)]

    def model_of(cols):
        return jnp.dot(a_wide, b_wide[:, cols], preferred_element_type=jnp.float32)

    later = model_of(pieces[0])
    part = len(pieces) // len(copies)
    for i, cols in enumerate(pieces):
        if i % part == 0:
            copies[i // part].wait()
        model = later
        if i + 1 < len(pieces):
            later = model_of(pieces[i + 1])
        guess = pltpu.reciprocal(model, approx=True)
        high, low = split(read(d_all, cols) * (guess * (2.0 - model * guess)))
        pair = b_pair[cols, :]
        total += jnp.dot(high, pair, preferred_element_type=jnp.float32)
        total += jnp.dot(low, pair, preferred_element_type=jnp.float32)
    numer = total[:, :k] + total[:, k:]
    each = rows // groups
    for g in range(groups):
        start = g * (each + pad)
        o_ref[pl.ds(start, each), :] = numer[g * each : (g + 1) * each]
        o_ref[pl.ds(start + each, pad), :] = b_sum


def half(fetch, read, d, d_shape, a, b, rows, groups, pad, which):
    n, k = b.shape
    whole = pl.BlockSpec(memory_space=pltpu.VMEM)
    return pl.pallas_call(
        functools.partial(half_kernel, fetch, read, groups, pad),
        in_specs=[pl.BlockSpec(memory_space=pltpu.SMEM), pl.BlockSpec(memory_space=pl.ANY), whole, whole],
        out_specs=whole,
        out_shape=jax.ShapeDtypeStruct((rows + groups * pad, k), jnp.float32),
        scratch_shapes=[
            pltpu.VMEM(d_shape, jnp.float32),
            pltpu.VMEM((3 * k, n), jnp.bfloat16),
            pltpu.VMEM((n, 2 * k), jnp.bfloat16),
            pltpu.SemaphoreType.DMA((H_COPIES,)),
        ],
        compiler_params=pltpu.CompilerParams(vmem_limit_bytes=VMEM),
        cost_estimate=pl.CostEstimate(flops=12 * rows * n * k, bytes_accessed=4 * rows * n, transcendentals=0),
    )(which, d, a, b)


def half_h(dt, h_panel, w_panel):
    n, k = h_panel.shape

    def fetch(which, ref, held, sems):
        width = ref.shape[1] // H_COPIES
        parts = [pl.ds(i * width, width) for i in range(H_COPIES)]
        return [pltpu.make_async_copy(ref.at[:, cols], held.at[:, cols], sems.at[i]) for i, cols in enumerate(parts)]

    def read(held, cols):
        return held[:, cols]

    first = jnp.zeros((1,), jnp.int32)
    return half(fetch, read, dt, dt.shape, h_panel, w_panel, n, X, H_PAD, first).reshape(X, -1, k)


def half_w(d5, w_panel, h_panel, core):
    rows, n = d5.shape[3], d5.shape[4]
    block = ZL * Y * rows

    def fetch(which, ref, held, sems):
        return [pltpu.make_async_copy(ref.at[:, :, which], held, sems.at[0])]

    def read(held, cols):
        return jnp.swapaxes(held[:, :, :, cols], 0, 1).reshape(block, -1)

    return half(fetch, read, d5, (Y, ZL, rows, n), w_panel, h_panel, block, ZL * Y, W_PAD, core)


def update_kernel(copies, parts_ref, w_ref, o_ref, *copies_ref):
    rows = w_ref.shape[0]
    each = rows + W_PAD
    total = parts_ref[pl.ds(0, each), :]
    for g in range(1, copies):
        total += parts_ref[pl.ds(g * each, each), :]
    w = w_ref[...] * total[:rows] / total[rows : rows + 1]
    o_ref[...] = w
    for ref in copies_ref:
        for g in range(copies):
            ref[g] = w


def update(parts, w, last):
    copies = ZL * Y
    whole = pl.BlockSpec(memory_space=pltpu.VMEM)
    shapes = [jax.ShapeDtypeStruct(w.shape, w.dtype)]
    if not last:
        shapes.append(jax.ShapeDtypeStruct((copies,) + w.shape, w.dtype))
    return pl.pallas_call(
        functools.partial(update_kernel, copies),
        in_specs=[whole, whole],
        out_specs=[whole] * len(shapes),
        out_shape=shapes,
        compiler_params=pltpu.CompilerParams(vmem_limit_bytes=VMEM),
    )(parts, w)


def turn_kernel(d_ref, o_ref):
    n = d_ref.shape[-1]
    o_ref[...] = d_ref[...].reshape(-1, n).T


def turned(d5):
    rows, n = d5.shape[3], d5.shape[4]
    return pl.pallas_call(
        turn_kernel,
        grid=(C * ZL,),
        in_specs=[pl.BlockSpec((Y, 1, 1, rows, n), lambda i: (0, i % ZL, i // ZL, 0, 0))],
        out_specs=pl.BlockSpec((n, Y * rows), lambda i: (0, i)),
        out_shape=jax.ShapeDtypeStruct((n, C * ZL * Y * rows), jnp.float32),
        compiler_params=pltpu.CompilerParams(vmem_limit_bytes=TURN_VMEM),
        cost_estimate=pl.CostEstimate(flops=0, bytes_accessed=8 * d5.size, transcendentals=0),
    )(d5)


def exchange(chunks, axes):
    return lax.all_to_all(chunks, axes, 0, 0, tiled=True)


def spread(part, axes, n):
    whole = exchange(jnp.broadcast_to(part[None], (n,) + part.shape), axes)
    return whole.reshape((-1,) + part.shape[1:])


def gather_w(copies):
    whole = exchange(copies, COL).reshape(-1, copies.shape[2])
    return lax.all_gather(whole, "c", axis=0, tiled=True)


def on_device(data, w, h):
    (w_rows, k), h_rows = w.shape, h.shape[0]
    d5 = data.reshape(Y, ZL, C, w_rows, data.shape[1])
    core = lax.axis_index("c").astype(jnp.int32).reshape(1)
    w_panel = gather_w(jnp.broadcast_to(w[None], (ZL * Y,) + w.shape))
    dt = turned(d5)
    h_x = lax.all_gather(h, "zh", axis=0, tiled=True)
    h_x, core, other = lax.optimization_barrier((h_x, core, 1 - core))
    h_panel = spread(h_x, "x", X)
    for step in range(ITERS):
        part = half_h(dt, h_panel, w_panel)
        part = jnp.sum(exchange(part, "x"), axis=0)
        part = jnp.sum(lax.all_gather(part, "zh", axis=0), axis=0)
        h_x = h_x * part[: ZH * h_rows] / part[ZH * h_rows]
        h_panel = spread(h_x, "x", X)
        sent = lax.ppermute(half_w(d5, w_panel, h_panel, other), "c", [(0, 1), (1, 0)])
        part = half_w(d5, w_panel, h_panel, core) + sent
        part = exchange(part.reshape(ZL * Y, 1, -1), COL).reshape(-1, k)
        last = step == ITERS - 1
        w, *copies = update(part, w, last)
        if not last:
            w_panel = gather_w(*copies)
    return w, lax.dynamic_slice_in_dim(h_x, lax.axis_index("zh") * h_rows, h_rows, 0)


def solution(mesh):
    fine = Mesh(mesh.devices.reshape(X, ZH, Y, ZL, C), ("x", "zh", "y", "zl", "c"))
    row, col = ("x", "zh"), ("y", "zl", "c")
    in_specs = (P(row, col), P(row + col, None), P(col + row, None))
    out_specs = (P(row + col, None), P(col + row, None))
    return jax.shard_map(on_device, mesh=fine, in_specs=in_specs, out_specs=out_specs, check_vma=False)
```

```python
import functools

import jax
import jax.numpy as jnp
from jax import lax
from jax.experimental import pallas as pl
from jax.experimental.pallas import tpu as pltpu
from jax.sharding import Mesh, PartitionSpec as P

ITERS = 2
X, ZH, Y, ZL, C = 4, 4, 8, 3, 2
COL = ("zl", "y")
H_PAD, W_PAD = 8, 1
PIECE = 256
VMEM, TURN_VMEM = 48 * 2**20, 60 * 2**20


def split(a):
    high = a.astype(jnp.bfloat16)
    return high, (a - high.astype(jnp.float32)).astype(jnp.bfloat16)


def half_kernel(fetch, read, groups, pad, which_ref, a_ref, b_ref, *refs):
    d_refs, (o_ref, d_all, b_wide, b_pair, sems) = refs[:-5], refs[-5:]
    n, k = b_ref.shape
    rows = o_ref.shape[0] - groups * pad
    which = which_ref[0]
    copies = fetch(which, d_refs, d_all, sems)
    for copy in copies:
        copy.start()
    b = b_ref[...]
    high, low = split(b.T)
    b_wide[...] = jnp.concatenate([high, high, low], axis=0)
    b_pair[...] = jnp.concatenate(split(b), axis=1)
    b_sum = jnp.broadcast_to(jnp.sum(b, axis=0, keepdims=True), (pad, k))
    high, low = split(a_ref[pl.ds(pl.multiple_of(which * rows, rows), rows), :])
    a_wide = jnp.concatenate([high, low, high], axis=1)
    total = jnp.zeros((rows, 2 * k), jnp.float32)
    pieces = [pl.ds(at, PIECE) for at in range(0, n, PIECE)]

    def model_of(cols):
        return jnp.dot(a_wide, b_wide[:, cols], preferred_element_type=jnp.float32)

    later = model_of(pieces[0])
    part = len(pieces) // len(copies)
    for i, cols in enumerate(pieces):
        if i % part == 0:
            copies[i // part].wait()
        model = later
        if i + 1 < len(pieces):
            later = model_of(pieces[i + 1])
        guess = pltpu.reciprocal(model, approx=True)
        high, low = split(read(d_all, cols) * (guess * (2.0 - model * guess)))
        pair = b_pair[cols, :]
        total += jnp.dot(high, pair, preferred_element_type=jnp.float32)
        total += jnp.dot(low, pair, preferred_element_type=jnp.float32)
    numer = total[:, :k] + total[:, k:]
    each = rows // groups
    for g in range(groups):
        start = g * (each + pad)
        o_ref[pl.ds(start, each), :] = numer[g * each : (g + 1) * each]
        o_ref[pl.ds(start + each, pad), :] = b_sum


def half(fetch, read, d, d_shape, a, b, rows, groups, pad, which):
    n, k = b.shape
    whole = pl.BlockSpec(memory_space=pltpu.VMEM)
    return pl.pallas_call(
        functools.partial(half_kernel, fetch, read, groups, pad),
        in_specs=[pl.BlockSpec(memory_space=pltpu.SMEM), whole, whole] + [pl.BlockSpec(memory_space=pl.ANY)] * len(d),
        out_specs=whole,
        out_shape=jax.ShapeDtypeStruct((rows + groups * pad, k), jnp.float32),
        scratch_shapes=[
            pltpu.VMEM(d_shape, jnp.float32),
            pltpu.VMEM((3 * k, n), jnp.bfloat16),
            pltpu.VMEM((n, 2 * k), jnp.bfloat16),
            pltpu.SemaphoreType.DMA((len(d),)),
        ],
        compiler_params=pltpu.CompilerParams(vmem_limit_bytes=VMEM),
        cost_estimate=pl.CostEstimate(flops=12 * rows * n * k, bytes_accessed=4 * rows * n, transcendentals=0),
    )(which, a, b, *d)


def half_h(dt, h_panel, w_panel):
    n, k = h_panel.shape

    def fetch(which, refs, held, sems):
        width = refs[0].shape[1]
        parts = [held.at[:, pl.ds(i * width, width)] for i in range(len(refs))]
        return [pltpu.make_async_copy(ref, part, sems.at[i]) for i, (ref, part) in enumerate(zip(refs, parts))]

    def read(held, cols):
        return held[:, cols]

    first = jnp.zeros((1,), jnp.int32)
    return half(fetch, read, dt, (n, w_panel.shape[0]), h_panel, w_panel, n, X, H_PAD, first).reshape(X, -1, k)


def half_w(d5, w_panel, h_panel, core):
    rows, n = d5.shape[3], d5.shape[4]
    block = ZL * Y * rows

    def fetch(which, refs, held, sems):
        return [pltpu.make_async_copy(refs[0].at[:, :, which], held, sems.at[0])]

    def read(held, cols):
        return jnp.swapaxes(held[:, :, :, cols], 0, 1).reshape(block, -1)

    return half(fetch, read, [d5], (Y, ZL, rows, n), w_panel, h_panel, block, ZL * Y, W_PAD, core)


def update_kernel(copies, parts_ref, w_ref, o_ref, *copies_ref):
    rows = w_ref.shape[0]
    each = rows + W_PAD
    total = parts_ref[pl.ds(0, each), :]
    for g in range(1, copies):
        total += parts_ref[pl.ds(g * each, each), :]
    w = w_ref[...] * total[:rows] / total[rows : rows + 1]
    o_ref[...] = w
    for ref in copies_ref:
        for g in range(copies):
            ref[g] = w


def update(parts, w, last):
    copies = ZL * Y
    whole = pl.BlockSpec(memory_space=pltpu.VMEM)
    shapes = [jax.ShapeDtypeStruct(w.shape, w.dtype)]
    if not last:
        shapes.append(jax.ShapeDtypeStruct((copies,) + w.shape, w.dtype))
    return pl.pallas_call(
        functools.partial(update_kernel, copies),
        in_specs=[whole, whole],
        out_specs=[whole] * len(shapes),
        out_shape=shapes,
        compiler_params=pltpu.CompilerParams(vmem_limit_bytes=VMEM),
    )(parts, w)


def turn_kernel(d_ref, *o_refs):
    n = d_ref.shape[-1]
    for c, o_ref in enumerate(o_refs):
        o_ref[...] = d_ref[:, 0, c].reshape(-1, n).T


def turned(d5):
    rows, n = d5.shape[3], d5.shape[4]
    return pl.pallas_call(
        turn_kernel,
        grid=(ZL,),
        in_specs=[pl.BlockSpec((Y, 1, C, rows, n), lambda i: (0, i, 0, 0, 0))],
        out_specs=[pl.BlockSpec((n, Y * rows), lambda i: (0, i))] * C,
        out_shape=[jax.ShapeDtypeStruct((n, ZL * Y * rows), jnp.float32)] * C,
        compiler_params=pltpu.CompilerParams(vmem_limit_bytes=TURN_VMEM),
        cost_estimate=pl.CostEstimate(flops=0, bytes_accessed=8 * d5.size, transcendentals=0),
    )(d5)


def exchange(chunks, axes):
    return lax.all_to_all(chunks, axes, 0, 0, tiled=True)


def spread(part, axes, n):
    whole = exchange(jnp.broadcast_to(part[None], (n,) + part.shape), axes)
    return whole.reshape((-1,) + part.shape[1:])


def gather_w(copies):
    whole = exchange(copies, COL).reshape(-1, copies.shape[2])
    return lax.all_gather(whole, "c", axis=0, tiled=True)


def on_device(data, w, h):
    (w_rows, k), h_rows = w.shape, h.shape[0]
    d5 = data.reshape(Y, ZL, C, w_rows, data.shape[1])
    core = lax.axis_index("c").astype(jnp.int32).reshape(1)
    w_panel = gather_w(jnp.broadcast_to(w[None], (ZL * Y,) + w.shape))
    dt = turned(d5)
    h_x = lax.all_gather(h, "zh", axis=0, tiled=True)
    h_x, core, other = lax.optimization_barrier((h_x, core, 1 - core))
    h_panel = spread(h_x, "x", X)
    for step in range(ITERS):
        part = half_h(dt, h_panel, w_panel)
        part = jnp.sum(exchange(part, "x"), axis=0)
        part = jnp.sum(lax.all_gather(part, "zh", axis=0), axis=0)
        h_x = h_x * part[: ZH * h_rows] / part[ZH * h_rows]
        h_panel = spread(h_x, "x", X)
        sent = lax.ppermute(half_w(d5, w_panel, h_panel, other), "c", [(0, 1), (1, 0)])
        part = half_w(d5, w_panel, h_panel, core) + sent
        part = exchange(part.reshape(ZL * Y, 1, -1), COL).reshape(-1, k)
        last = step == ITERS - 1
        w, *copies = update(part, w, last)
        if not last:
            w_panel = gather_w(*copies)
    return w, lax.dynamic_slice_in_dim(h_x, lax.axis_index("zh") * h_rows, h_rows, 0)


def solution(mesh):
    fine = Mesh(mesh.devices.reshape(X, ZH, Y, ZL, C), ("x", "zh", "y", "zl", "c"))
    row, col = ("x", "zh"), ("y", "zl", "c")
    in_specs = (P(row, col), P(row + col, None), P(col + row, None))
    out_specs = (P(row + col, None), P(col + row, None))
    return jax.shard_map(on_device, mesh=fine, in_specs=in_specs, out_specs=out_specs, check_vma=False)
```

```python
import functools

import jax
import jax.numpy as jnp
from jax import lax
from jax.experimental import pallas as pl
from jax.experimental.pallas import tpu as pltpu
from jax.sharding import Mesh, PartitionSpec as P

ITERS = 2
X, ZH, Y, ZL, C = 4, 4, 8, 3, 2
COL = ("zl", "y")
H_PAD, W_PAD = 8, 1
PIECE = 256
VMEM, FIRST_VMEM, MOST_VMEM = 48 * 2**20, 51 * 2**20, 60 * 2**20


def split(a):
    high = a.astype(jnp.bfloat16)
    return high, (a - high.astype(jnp.float32)).astype(jnp.bfloat16)


def half_kernel(fetch, read, groups, pad, which_ref, a_ref, b_ref, *refs):
    d_refs, (o_ref, d_all, b_wide, b_pair, sems) = refs[:-5], refs[-5:]
    n, k = b_ref.shape
    rows = o_ref.shape[0] - groups * pad
    which = which_ref[0]
    copies = fetch(which, d_refs, d_all, sems)
    for copy in copies:
        copy.start()
    b = b_ref[...]
    high, low = split(b.T)
    b_wide[...] = jnp.concatenate([high, high, low], axis=0)
    b_pair[...] = jnp.concatenate(split(b), axis=1)
    b_sum = jnp.broadcast_to(jnp.sum(b, axis=0, keepdims=True), (pad, k))
    high, low = split(a_ref[pl.ds(pl.multiple_of(which * rows, rows), rows), :])
    a_wide = jnp.concatenate([high, low, high], axis=1)
    total = jnp.zeros((rows, 2 * k), jnp.float32)
    pieces = [pl.ds(at, PIECE) for at in range(0, n, PIECE)]

    def model_of(cols):
        return jnp.dot(a_wide, b_wide[:, cols], preferred_element_type=jnp.float32)

    later = model_of(pieces[0])
    part = len(pieces) // len(copies)
    for i, cols in enumerate(pieces):
        if i % part == 0:
            copies[i // part].wait()
        model = later
        if i + 1 < len(pieces):
            later = model_of(pieces[i + 1])
        guess = pltpu.reciprocal(model, approx=True)
        high, low = split(read(d_all, cols) * (guess * (2.0 - model * guess)))
        pair = b_pair[cols, :]
        total += jnp.dot(high, pair, preferred_element_type=jnp.float32)
        total += jnp.dot(low, pair, preferred_element_type=jnp.float32)
    numer = total[:, :k] + total[:, k:]
    each = rows // groups
    for g in range(groups):
        start = g * (each + pad)
        o_ref[pl.ds(start, each), :] = numer[g * each : (g + 1) * each]
        o_ref[pl.ds(start + each, pad), :] = b_sum


def half(fetch, read, d, d_shape, a, b, rows, groups, pad, which, limit=VMEM):
    n, k = b.shape
    whole = pl.BlockSpec(memory_space=pltpu.VMEM)
    return pl.pallas_call(
        functools.partial(half_kernel, fetch, read, groups, pad),
        in_specs=[pl.BlockSpec(memory_space=pltpu.SMEM), whole, whole] + [pl.BlockSpec(memory_space=pl.ANY)] * len(d),
        out_specs=whole,
        out_shape=jax.ShapeDtypeStruct((rows + groups * pad, k), jnp.float32),
        scratch_shapes=[
            pltpu.VMEM(d_shape, jnp.float32),
            pltpu.VMEM((3 * k, n), jnp.bfloat16),
            pltpu.VMEM((n, 2 * k), jnp.bfloat16),
            pltpu.SemaphoreType.DMA((len(d),)),
        ],
        compiler_params=pltpu.CompilerParams(vmem_limit_bytes=limit),
        cost_estimate=pl.CostEstimate(flops=12 * rows * n * k, bytes_accessed=4 * rows * n, transcendentals=0),
    )(which, a, b, *d)


def half_h(dt, h_panel, w_panel, limit):
    n, k = h_panel.shape

    def fetch(which, refs, held, sems):
        width = refs[0].shape[1]
        parts = [held.at[:, pl.ds(i * width, width)] for i in range(len(refs))]
        return [pltpu.make_async_copy(ref, part, sems.at[i]) for i, (ref, part) in enumerate(zip(refs, parts))]

    def read(held, cols):
        return held[:, cols]

    first = jnp.zeros((1,), jnp.int32)
    return half(fetch, read, dt, (n, w_panel.shape[0]), h_panel, w_panel, n, X, H_PAD, first, limit).reshape(X, -1, k)


def half_w(d5, w_panel, h_panel, core):
    rows, n = d5.shape[3], d5.shape[4]
    block = ZL * Y * rows

    def fetch(which, refs, held, sems):
        return [pltpu.make_async_copy(refs[0].at[:, :, which], held, sems.at[0])]

    def read(held, cols):
        return jnp.swapaxes(held[:, :, :, cols], 0, 1).reshape(block, -1)

    return half(fetch, read, [d5], (Y, ZL, rows, n), w_panel, h_panel, block, ZL * Y, W_PAD, core)


def update_kernel(copies, parts_ref, w_ref, o_ref, *copies_ref):
    rows = w_ref.shape[0]
    each = rows + W_PAD
    total = parts_ref[pl.ds(0, each), :]
    for g in range(1, copies):
        total += parts_ref[pl.ds(g * each, each), :]
    w = w_ref[...] * total[:rows] / total[rows : rows + 1]
    o_ref[...] = w
    for ref in copies_ref:
        for g in range(copies):
            ref[g] = w


def update(parts, w, last):
    copies = ZL * Y
    whole = pl.BlockSpec(memory_space=pltpu.VMEM)
    shapes = [jax.ShapeDtypeStruct(w.shape, w.dtype)]
    if not last:
        shapes.append(jax.ShapeDtypeStruct((copies,) + w.shape, w.dtype))
    return pl.pallas_call(
        functools.partial(update_kernel, copies),
        in_specs=[whole, whole],
        out_specs=[whole] * len(shapes),
        out_shape=shapes,
        compiler_params=pltpu.CompilerParams(vmem_limit_bytes=VMEM),
    )(parts, w)


def turn_kernel(d_ref, *o_refs):
    n = d_ref.shape[-1]
    for c, o_ref in enumerate(o_refs):
        o_ref[...] = d_ref[:, 0, c].reshape(-1, n).T


def turned(d5):
    rows, n = d5.shape[3], d5.shape[4]
    return pl.pallas_call(
        turn_kernel,
        grid=(ZL,),
        in_specs=[pl.BlockSpec((Y, 1, C, rows, n), lambda i: (0, i, 0, 0, 0))],
        out_specs=[pl.BlockSpec((n, Y * rows), lambda i: (0, i))] * C,
        out_shape=[jax.ShapeDtypeStruct((n, ZL * Y * rows), jnp.float32)] * C,
        compiler_params=pltpu.CompilerParams(vmem_limit_bytes=MOST_VMEM),
        cost_estimate=pl.CostEstimate(flops=0, bytes_accessed=8 * d5.size, transcendentals=0),
    )(d5)


def exchange(chunks, axes):
    return lax.all_to_all(chunks, axes, 0, 0, tiled=True)


def spread(part, axes, n):
    whole = exchange(jnp.broadcast_to(part[None], (n,) + part.shape), axes)
    return whole.reshape((-1,) + part.shape[1:])


def gather_w(copies):
    whole = exchange(copies, COL).reshape(-1, copies.shape[2])
    return lax.all_gather(whole, "c", axis=0, tiled=True)


def on_device(data, w, h):
    (w_rows, k), h_rows = w.shape, h.shape[0]
    d5 = data.reshape(Y, ZL, C, w_rows, data.shape[1])
    core = lax.axis_index("c").astype(jnp.int32).reshape(1)
    w_panel = gather_w(jnp.broadcast_to(w[None], (ZL * Y,) + w.shape))
    dt = turned(d5)
    h_x = lax.all_gather(h, "zh", axis=0, tiled=True)
    h_x, core, other = lax.optimization_barrier((h_x, core, 1 - core))
    h_panel = spread(h_x, "x", X)
    for step in range(ITERS):
        part = half_h(dt, h_panel, w_panel, FIRST_VMEM if step == 0 else VMEM)
        part = jnp.sum(exchange(part, "x"), axis=0)
        part = jnp.sum(lax.all_gather(part, "zh", axis=0), axis=0)
        h_x = h_x * part[: ZH * h_rows] / part[ZH * h_rows]
        h_panel = spread(h_x, "x", X)
        sent = lax.ppermute(half_w(d5, w_panel, h_panel, other), "c", [(0, 1), (1, 0)])
        part = half_w(d5, w_panel, h_panel, core) + sent
        part = exchange(part.reshape(ZL * Y, 1, -1), COL).reshape(-1, k)
        last = step == ITERS - 1
        w, *copies = update(part, w, last)
        if not last:
            w_panel = gather_w(*copies)
    return w, lax.dynamic_slice_in_dim(h_x, lax.axis_index("zh") * h_rows, h_rows, 0)


def solution(mesh):
    fine = Mesh(mesh.devices.reshape(X, ZH, Y, ZL, C), ("x", "zh", "y", "zl", "c"))
    row, col = ("x", "zh"), ("y", "zl", "c")
    in_specs = (P(row, col), P(row + col, None), P(col + row, None))
    out_specs = (P(row + col, None), P(col + row, None))
    return jax.shard_map(on_device, mesh=fine, in_specs=in_specs, out_specs=out_specs, check_vma=False)
```

```python
import functools

import jax
import jax.numpy as jnp
from jax import lax
from jax.experimental import pallas as pl
from jax.experimental.pallas import tpu as pltpu
from jax.sharding import Mesh, PartitionSpec as P

ITERS = 2
X, ZH, Y, ZL, C = 4, 4, 8, 3, 2
COL = ("zl", "y")
H_PAD, W_PAD = 8, 1
PIECE = 256
VMEM, NEXT_VMEM, FIRST_VMEM, MOST_VMEM = 48 * 2**20, 36 * 2**20, 51 * 2**20, 60 * 2**20


def split(a):
    high = a.astype(jnp.bfloat16)
    return high, (a - high.astype(jnp.float32)).astype(jnp.bfloat16)


def half_kernel(fetch, read, groups, pad, which_ref, a_ref, b_ref, *refs):
    d_refs, (o_ref, d_all, b_wide, b_pair, sems) = refs[:-5], refs[-5:]
    n, k = b_ref.shape
    rows = o_ref.shape[0] - groups * pad
    which = which_ref[0]
    copies = fetch(which, d_refs, d_all, sems)
    for copy in copies:
        copy.start()
    b = b_ref[...]
    high, low = split(b.T)
    b_wide[...] = jnp.concatenate([high, high, low], axis=0)
    b_pair[...] = jnp.concatenate(split(b), axis=1)
    b_sum = jnp.broadcast_to(jnp.sum(b, axis=0, keepdims=True), (pad, k))
    high, low = split(a_ref[pl.ds(pl.multiple_of(which * rows, rows), rows), :])
    a_wide = jnp.concatenate([high, low, high], axis=1)
    total = jnp.zeros((rows, 2 * k), jnp.float32)
    pieces = [pl.ds(at, PIECE) for at in range(0, n, PIECE)]

    def model_of(cols):
        return jnp.dot(a_wide, b_wide[:, cols], preferred_element_type=jnp.float32)

    later = model_of(pieces[0])
    part = len(pieces) // len(copies)
    for i, cols in enumerate(pieces):
        if i % part == 0:
            copies[i // part].wait()
        model = later
        if i + 1 < len(pieces):
            later = model_of(pieces[i + 1])
        guess = pltpu.reciprocal(model, approx=True)
        high, low = split(read(d_all, cols) * (guess * (2.0 - model * guess)))
        pair = b_pair[cols, :]
        total += jnp.dot(high, pair, preferred_element_type=jnp.float32)
        total += jnp.dot(low, pair, preferred_element_type=jnp.float32)
    numer = total[:, :k] + total[:, k:]
    each = rows // groups
    for g in range(groups):
        start = g * (each + pad)
        o_ref[pl.ds(start, each), :] = numer[g * each : (g + 1) * each]
        o_ref[pl.ds(start + each, pad), :] = b_sum


def half(fetch, read, d, d_shape, a, b, rows, groups, pad, which, limit=VMEM):
    n, k = b.shape
    whole = pl.BlockSpec(memory_space=pltpu.VMEM)
    return pl.pallas_call(
        functools.partial(half_kernel, fetch, read, groups, pad),
        in_specs=[pl.BlockSpec(memory_space=pltpu.SMEM), whole, whole] + [pl.BlockSpec(memory_space=pl.ANY)] * len(d),
        out_specs=whole,
        out_shape=jax.ShapeDtypeStruct((rows + groups * pad, k), jnp.float32),
        scratch_shapes=[
            pltpu.VMEM(d_shape, jnp.float32),
            pltpu.VMEM((3 * k, n), jnp.bfloat16),
            pltpu.VMEM((n, 2 * k), jnp.bfloat16),
            pltpu.SemaphoreType.DMA((len(d),)),
        ],
        compiler_params=pltpu.CompilerParams(vmem_limit_bytes=limit),
        cost_estimate=pl.CostEstimate(flops=12 * rows * n * k, bytes_accessed=4 * rows * n, transcendentals=0),
    )(which, a, b, *d)


def half_h(dt, h_panel, w_panel, limit):
    n, k = h_panel.shape

    def fetch(which, refs, held, sems):
        width = refs[0].shape[1]
        parts = [held.at[:, pl.ds(i * width, width)] for i in range(len(refs))]
        return [pltpu.make_async_copy(ref, part, sems.at[i]) for i, (ref, part) in enumerate(zip(refs, parts))]

    def read(held, cols):
        return held[:, cols]

    first = jnp.zeros((1,), jnp.int32)
    return half(fetch, read, dt, (n, w_panel.shape[0]), h_panel, w_panel, n, X, H_PAD, first, limit).reshape(X, -1, k)


def half_w(d5, w_panel, h_panel, core):
    rows, n = d5.shape[3], d5.shape[4]
    block = ZL * Y * rows

    def fetch(which, refs, held, sems):
        return [pltpu.make_async_copy(refs[0].at[:, :, which], held, sems.at[0])]

    def read(held, cols):
        return jnp.swapaxes(held[:, :, :, cols], 0, 1).reshape(block, -1)

    return half(fetch, read, [d5], (Y, ZL, rows, n), w_panel, h_panel, block, ZL * Y, W_PAD, core)


def update_kernel(copies, parts_ref, w_ref, o_ref, *copies_ref):
    rows = w_ref.shape[0]
    each = rows + W_PAD
    total = parts_ref[pl.ds(0, each), :]
    for g in range(1, copies):
        total += parts_ref[pl.ds(g * each, each), :]
    w = w_ref[...] * total[:rows] / total[rows : rows + 1]
    o_ref[...] = w
    for ref in copies_ref:
        for g in range(copies):
            ref[g] = w


def update(parts, w, last):
    copies = ZL * Y
    whole = pl.BlockSpec(memory_space=pltpu.VMEM)
    shapes = [jax.ShapeDtypeStruct(w.shape, w.dtype)]
    if not last:
        shapes.append(jax.ShapeDtypeStruct((copies,) + w.shape, w.dtype))
    return pl.pallas_call(
        functools.partial(update_kernel, copies),
        in_specs=[whole, whole],
        out_specs=[whole] * len(shapes),
        out_shape=shapes,
        compiler_params=pltpu.CompilerParams(vmem_limit_bytes=VMEM),
    )(parts, w)


def turn_kernel(d_ref, *o_refs):
    n = d_ref.shape[-1]
    for c, o_ref in enumerate(o_refs):
        o_ref[...] = d_ref[:, 0, c].reshape(-1, n).T


def turned(d5):
    rows, n = d5.shape[3], d5.shape[4]
    return pl.pallas_call(
        turn_kernel,
        grid=(ZL,),
        in_specs=[pl.BlockSpec((Y, 1, C, rows, n), lambda i: (0, i, 0, 0, 0))],
        out_specs=[pl.BlockSpec((n, Y * rows), lambda i: (0, i))] * C,
        out_shape=[jax.ShapeDtypeStruct((n, ZL * Y * rows), jnp.float32)] * C,
        compiler_params=pltpu.CompilerParams(vmem_limit_bytes=MOST_VMEM),
        cost_estimate=pl.CostEstimate(flops=0, bytes_accessed=8 * d5.size, transcendentals=0),
    )(d5)


def exchange(chunks, axes):
    return lax.all_to_all(chunks, axes, 0, 0, tiled=True)


def spread(part, axes, n):
    whole = exchange(jnp.broadcast_to(part[None], (n,) + part.shape), axes)
    return whole.reshape((-1,) + part.shape[1:])


def gather_w(copies):
    whole = exchange(copies, COL).reshape(-1, copies.shape[2])
    return lax.all_gather(whole, "c", axis=0, tiled=True)


def on_device(data, w, h):
    (w_rows, k), h_rows = w.shape, h.shape[0]
    d5 = data.reshape(Y, ZL, C, w_rows, data.shape[1])
    core = lax.axis_index("c").astype(jnp.int32).reshape(1)
    w_panel = gather_w(jnp.broadcast_to(w[None], (ZL * Y,) + w.shape))
    dt = turned(d5)
    h_x = lax.all_gather(h, "zh", axis=0, tiled=True)
    h_x, core, other = lax.optimization_barrier((h_x, core, 1 - core))
    h_panel = spread(h_x, "x", X)
    for step in range(ITERS):
        part = half_h(dt, h_panel, w_panel, FIRST_VMEM if step == 0 else NEXT_VMEM)
        part = jnp.sum(exchange(part, "x"), axis=0)
        part = jnp.sum(lax.all_gather(part, "zh", axis=0), axis=0)
        h_x = h_x * part[: ZH * h_rows] / part[ZH * h_rows]
        h_panel = spread(h_x, "x", X)
        sent = lax.ppermute(half_w(d5, w_panel, h_panel, other), "c", [(0, 1), (1, 0)])
        part = half_w(d5, w_panel, h_panel, core) + sent
        part = exchange(part.reshape(ZL * Y, 1, -1), COL).reshape(-1, k)
        last = step == ITERS - 1
        w, *copies = update(part, w, last)
        if not last:
            w_panel = gather_w(*copies)
    return w, lax.dynamic_slice_in_dim(h_x, lax.axis_index("zh") * h_rows, h_rows, 0)


def solution(mesh):
    fine = Mesh(mesh.devices.reshape(X, ZH, Y, ZL, C), ("x", "zh", "y", "zl", "c"))
    row, col = ("x", "zh"), ("y", "zl", "c")
    in_specs = (P(row, col), P(row + col, None), P(col + row, None))
    out_specs = (P(row + col, None), P(col + row, None))
    return jax.shard_map(on_device, mesh=fine, in_specs=in_specs, out_specs=out_specs, check_vma=False)
```
